32 devices in a mesh: group: 1, ctx: 32 (over z, y, x, core), tp: 1.
Axes of the slice: x: 2, y: 2, z: 4, core: 2. Of those that a mesh axis runs over, the one named last changes fastest.
Arguments:
- hidden_in: bfloat16 [4096, 4096], P(('group', 'ctx'), 'tp'), may hold values from -6 to 6
- route: int32 [4096], P(('group', 'ctx')), may hold values from 0 to 4095, as said below
- queries: bfloat16 [4096, 768], P(('group', 'ctx'), 'tp'), may hold values from -400 to 400
- keys_values: bfloat16 [4096, 256], P(('group', 'ctx')), may hold values from -5 to 5
- ancestors: int32 [32, 16], P(('group', 'ctx')), may hold values from -1 to 31, as said below
- segments: int32 [4096], P(('group', 'ctx')), may hold values from 0 to 127, never falling along the last dimension, each value on 1 to 64 neighbouring positions
- w_out: bfloat16 [768, 4096], P('tp'), may hold values from -0.21875 to 0.21875
- w_score: float32 [4096], P('tp'), may hold values from -0.09375 to 0.09375
Outputs:
- hidden_out: bfloat16 [4096, 4096], P(('group', 'ctx'), 'tp')
- token_scores: float32 [4096], P(('group', 'ctx'))
The draws below stay inside these ranges and needn't reach their ends.
Inputs may be any that keep to these rules, and one draw needn't show every extreme that they name: route is a permutation of the context positions. The 128 rows of one loader shard send at most 5 rows to each context shard (positions of one block of 128), and some pair reaches 5; each context shard receives 128 rows. Within a context shard, positions follow the loader shard's index and then the row's index in it. `ancestors`: row b lists 1 to 16 distinct blocks other than b, then -1 to the end; some row lists 16.
All inputs are finite; a program needn't handle non-finite values.
Results may differ from the reference program's by a relative error of at most 0.005.
Values may be sent and summed in bfloat16 or wider, within the bound.
A program may use at most 64 MiB of HBM per device.

```python
import math
import jax
import jax.numpy as jnp
import numpy as np
from jax import lax

D = 4096
QH = 6
HEAD = 128
BLOCK = 128
MAXB = 16
TOK_DEV = 128
TOKENS = 4096


def tree_lists(key):
    block_count = TOKENS // BLOCK
    base_key = jax.random.fold_in(key, 7001)
    count_key, pick_key, perm_key = jax.random.split(base_key, 3)
    counts = jax.random.randint(count_key, (block_count,), 1, MAXB + 1)
    chosen = jax.random.randint(pick_key, (), 0, block_count)
    counts = jnp.where(jnp.arange(block_count) == chosen, MAXB, counts)
    perm_keys = jax.random.split(perm_key, block_count)
    others = jax.vmap(lambda one_key: jax.random.permutation(one_key, block_count - 1)[:MAXB])(perm_keys)
    own_block = jnp.arange(block_count)[:, None]
    named_blocks = others + (others >= own_block).astype(others.dtype)
    column = jnp.arange(MAXB)[None, :]
    return jnp.where(column < counts[:, None], named_blocks, -1).astype(jnp.int32)


def draw_route(key, part):
    shards = TOKENS // TOK_DEV
    base_key = jax.random.fold_in(key, 7005)
    key_order, key_rows = jax.random.split(base_key)
    order_of = jax.random.permutation(key_order, shards)
    offsets = jnp.arange(TOK_DEV) % shards
    offsets = offsets.at[1].set(0)
    loaders = jnp.arange(shards)
    dest_shard = order_of[(loaders[:, None] + offsets[None, :]) % shards]
    row_keys = jax.random.split(key_rows, shards)
    dest_shard = jax.vmap(lambda one_key, dest_row: jax.random.permutation(one_key, dest_row))(row_keys, dest_shard)
    flat_dest = dest_shard.reshape(-1)
    sorted_at = jnp.argsort(flat_dest, stable=True)
    return jnp.zeros((TOKENS,), jnp.int32).at[sorted_at].set(jnp.arange(TOKENS, dtype=jnp.int32))


def draw_ancestors(key, part):
    return tree_lists(key)


def draw_queries(key, part):
    values_drawn = jnp.clip(jax.random.normal(jax.random.fold_in(key, 7003), (TOKENS, QH * HEAD), jnp.float32), -4.0, 4.0)
    return values_drawn.astype(jnp.bfloat16)


def draw_keys_values(key, part):
    values_drawn = jnp.clip(jax.random.normal(jax.random.fold_in(key, 7004), (TOKENS, 2 * HEAD), jnp.float32), -4.0, 4.0)
    return values_drawn.astype(jnp.bfloat16)


def block_levels(stream_key, shape, pieces, least, largest):
    def one(dim, parts):
        draws = jax.random.uniform(jax.random.fold_in(jax.random.fold_in(stream_key, 6), dim), (parts,), jnp.float32, least / len(pieces), largest / len(pieces))
        return jnp.repeat(jnp.exp(draws), shape[dim] // parts).reshape((-1,) + (1,) * (len(shape) - dim - 1))

    loudness = one(*pieces[0])
    for cut in pieces[1:]:
        loudness = loudness * one(*cut)
    return loudness


def length_profile(count, total, limit, lean):
    loads = [(1 << 20) // math.isqrt(rank ** lean) + 1 for rank in range(2, count + 1)]
    surplus, given = total - limit - (count - 1), [1] * (count - 1)
    while surplus > 0:
        candidates = [i for i in range(count - 1) if given[i] < limit]
        pool, budget = sum([loads[i] for i in candidates]), surplus
        for i in candidates:
            extra = min(limit - given[i], max(1, budget * loads[i] // pool), surplus)
            given[i] = given[i] + extra
            surplus = surplus - extra
    return np.array([limit] + given)


def ragged(stream_key, count, total, bound, lean):
    if count == 2:
        one = jax.random.randint(stream_key, (), max(1, total - bound), min(bound, total - 1) + 1)
        return jnp.stack([one, total - one])
    sizes = jnp.asarray(length_profile(count, total, bound, lean), jnp.int32)
    twos = (count - 1) // 2
    source_of, receiver = sizes[1:1 + 2 * twos:2], sizes[2:2 + 2 * twos:2]
    slack = jnp.minimum(source_of - 1, bound - receiver)
    shifted = jax.random.randint(jax.random.fold_in(stream_key, 1), (twos,), 0, 1 << 20) % (slack + 1)
    sizes = sizes.at[1:1 + 2 * twos:2].set(source_of - shifted).at[2:2 + 2 * twos:2].set(receiver + shifted)
    return sizes[jax.random.permutation(jax.random.fold_in(stream_key, 2), count)]


def scatter_about(key, shape, scale, most, pieces=(), kind=jnp.bfloat16):
    factor_of = block_levels(key, shape, pieces, -0.22, 0.18) if pieces else 1.0
    result = jax.random.normal(key, shape, jnp.float32) * scale * factor_of
    return jnp.minimum(jnp.maximum(result, -most), most).astype(kind)


def setup_inputs(seed: int = 0, part: int = 0) -> dict:
    key_list = jax.random.split(jax.random.key(seed), 9)
    own_keys = jax.random.split(jax.random.fold_in(key_list[8], part), 9)
    hidden_in = scatter_about(own_keys[0], (TOKENS, D), 1.0, 6.0, ((0, 32),))
    route = draw_route(jax.random.fold_in(jax.random.fold_in(key_list[8], part), 71), part)
    queries = draw_queries(jax.random.fold_in(jax.random.fold_in(key_list[8], part), 71), part)
    keys_values = draw_keys_values(jax.random.fold_in(jax.random.fold_in(key_list[8], part), 71), part)
    ancestors = draw_ancestors(jax.random.fold_in(jax.random.fold_in(key_list[8], part), 71), part)
    segments = jnp.searchsorted(jnp.cumsum(ragged(own_keys[5], TOKENS // 32, TOKENS, 64, 2)), jnp.arange(TOKENS), side="right").astype(jnp.int32)
    w_out = scatter_about(key_list[6], (QH * HEAD, D), (QH * HEAD) ** -0.5, 0.21875)
    w_score = scatter_about(key_list[7], (D,), D ** -0.5, 0.09375, (), jnp.float32)
    return {"hidden_in": hidden_in, "route": route, "queries": queries, "keys_values": keys_values, "ancestors": ancestors, "segments": segments, "w_out": w_out, "w_score": w_score}


neg_big = -1e+30

def reference(hidden_in, route, queries, keys_values, ancestors, segments, w_out, w_score):
    hidden_ctx = jnp.zeros_like(hidden_in).at[route].set(hidden_in)
    block_count = TOKENS // BLOCK
    logit_scale = 1.0 / math.sqrt(HEAD)
    query_blocks = queries.reshape(block_count, BLOCK, QH, HEAD)
    pair_blocks = keys_values.reshape(block_count, BLOCK, 2 * HEAD)
    seg_blocks = segments.reshape(block_count, BLOCK)
    position = jnp.arange(BLOCK)
    causal = position[None, :] <= position[:, None]

    def attend_block(block_id):
        query_rows = query_blocks[block_id].astype(jnp.float32)
        listed = ancestors[block_id]
        safe_index = jnp.maximum(listed, 0)
        key_rows = jnp.concatenate([pair_blocks[block_id][None], pair_blocks[safe_index]], axis=0)
        key_rows = key_rows.reshape((MAXB + 1) * BLOCK, 2 * HEAD).astype(jnp.float32)
        seg_here = seg_blocks[block_id]
        own_mask = causal & (seg_here[None, :] == seg_here[:, None])
        far_mask = jnp.broadcast_to(jnp.repeat(listed >= 0, BLOCK)[None, :], (BLOCK, MAXB * BLOCK))
        visible = jnp.concatenate([own_mask, far_mask], axis=1)
        logits = jnp.einsum('thd,kd->htk', query_rows, key_rows[:, :HEAD]) * logit_scale
        logits = jnp.where(visible[None], logits, neg_big)
        row_max = lax.optimization_barrier(jnp.max(logits, axis=2, keepdims=True))
        weights_raw = jnp.exp(logits - row_max)
        row_total = lax.optimization_barrier(jnp.sum(weights_raw, axis=2))
        weights_held = lax.optimization_barrier(weights_raw.astype(jnp.bfloat16)).astype(jnp.float32)
        numerator = jnp.einsum('htk,kd->thd', weights_held, key_rows[:, HEAD:])
        return (numerator / jnp.transpose(row_total)[:, :, None]).astype(jnp.bfloat16)
    attended = lax.map(attend_block, jnp.arange(block_count).astype(jnp.int32))
    attended = attended.reshape(TOKENS, QH * HEAD)
    projected = jnp.dot(attended, w_out, preferred_element_type=jnp.float32)
    hidden_out = (hidden_ctx.astype(jnp.float32) + projected).astype(jnp.bfloat16)
    token_scores = lax.optimization_barrier(jnp.sum(hidden_out.astype(jnp.float32) * w_score[None, :], axis=1))
    return (hidden_out, token_scores)
```

```python
import functools
import math

import jax
import jax.numpy as jnp
from jax import lax
from jax.experimental import pallas as pl
from jax.experimental.pallas import tpu as pltpu
from jax.sharding import PartitionSpec as P

HEAD = 128
BLOCK = 128
EMPTY = 64.0


neg_big = -1e30


def partner(me, stride):
    return me + stride * (1 - 2 * ((me // stride) % 2))


def attend(anc_ref, q_ref, own_ref, bias_ref, far_ref, kv_all, k_cat, v_cat, att_ref):
    listed = anc_ref.shape[1]
    k_cat[0:BLOCK, :] = own_ref[:, :HEAD]
    v_cat[0:BLOCK, :] = own_ref[:, HEAD:]
    for j in range(listed):
        block = kv_all[jnp.maximum(anc_ref[0, j], 0)]
        rows = slice((j + 1) * BLOCK, (j + 2) * BLOCK)
        k_cat[rows, :] = block[:, :HEAD]
        v_cat[rows, :] = block[:, HEAD:]
    scale = 1.0 / math.sqrt(HEAD)
    for h in range(q_ref.shape[1] // HEAD):
        cols = slice(h * HEAD, (h + 1) * HEAD)
        logits = lax.dot_general(
            q_ref[:, cols],
            k_cat[...],
            (((1,), (1,)), ((), ())),
            preferred_element_type=jnp.float32,
        )
        near = logits[:, :BLOCK] * scale + bias_ref[...]
        far = logits[:, BLOCK:] * scale + far_ref[...]
        logits = jnp.concatenate([near, far], axis=1)
        top = jnp.max(logits, axis=1, keepdims=True)
        terms = jnp.exp(logits - top)
        total = jnp.sum(terms, axis=1, keepdims=True)
        weighted = jnp.dot(
            terms.astype(jnp.bfloat16), v_cat[...], preferred_element_type=jnp.float32
        )
        att_ref[:, cols] = (weighted / total).astype(jnp.bfloat16)


def kernel(
    n,
    anc_ref,
    q_ref,
    own_ref,
    bias_ref,
    far_ref,
    out_ref,
    w_ref,
    arrived_ref,
    proj_ref,
    kv_all,
    k_cat,
    v_cat,
    att_ref,
    w_vmem,
    w_sem,
    mine_sem,
    h_send,
    h_recv,
    z_send,
    f_send,
    kv_recv,
):
    me = lax.axis_index("ctx")
    lead = n // 8
    low = me % 8
    z = me // 8
    core = me % 2
    stride2 = 4 - 2 * core
    stride3 = 2 + 2 * core
    peers = (partner(me, stride2), partner(me, stride3), partner(me, 1))

    w_copy = pltpu.make_async_copy(w_ref, w_vmem, w_sem)
    w_copy.start()
    mine = pltpu.make_async_copy(out_ref.at[me], arrived_ref.at[me], mine_sem)
    mine.start()
    kv_all[me] = own_ref[...]

    barrier = pltpu.get_barrier_semaphore()

    @pl.loop(1, n)
    def _(d):
        pl.semaphore_signal(barrier, inc=1, device_id={"ctx": (me + d) % n})

    pl.semaphore_wait(barrier, n - 1)

    def hidden_copy(d):
        to = (me + d) % n
        return pltpu.make_async_remote_copy(
            src_ref=out_ref.at[to],
            dst_ref=arrived_ref.at[me],
            send_sem=h_send.at[d],
            recv_sem=h_recv.at[me],
            device_id={"ctx": to},
        )

    def send_hidden(first, count):
        @pl.loop(0, count)
        def _(i):
            hidden_copy(first + i).start()

    def kv_copy(block, send_sem, to):
        return pltpu.make_async_remote_copy(
            src_ref=kv_all.at[block],
            dst_ref=kv_all.at[block],
            send_sem=send_sem,
            recv_sem=kv_recv.at[block],
            device_id={"ctx": to},
        )

    def arrive(block):
        kv_copy(block, z_send.at[0], peers[2]).wait_recv()

    def forward(block, hops):
        for hop in hops:
            kv_copy(block, f_send.at[hop, block], peers[hop]).start()

    @pl.loop(1, lead)
    def _(l):
        kv_copy(me, z_send.at[l], ((z + l) % lead) * 8 + low).start()

    forward(me, (0, 1, 2))

    total = n - 1
    at_start = total // 4
    each = (total - at_start) // (2 * lead)
    second = 1 + at_start + each * (lead - 1)
    third = second + each * lead
    send_hidden(1, at_start)

    @pl.loop(1, lead)
    def _(l):
        block = ((z + l) % lead) * 8 + low
        arrive(block)
        forward(block, (0, 1, 2))
        send_hidden(1 + at_start + each * (l - 1), each)

    @pl.loop(0, lead)
    def _(l):
        block = ((z + l) % lead) * 8 + peers[0] % 8
        arrive(block)
        forward(block, (1, 2))
        send_hidden(second + each * l, each)

    send_hidden(third, n - third)
    across = peers[1]

    @pl.loop(0, lead)
    def _(l):
        block = ((z + l) % lead) * 8 + across % 8
        arrive(block)
        forward(block, (2,))

    across2 = partner(across, stride2)

    @pl.loop(0, lead)
    def _(l):
        block = ((z + l) % lead) * 8 + across2 % 8
        arrive(block)
        forward(block, (2,))

    @pl.loop(0, n // 2)
    def _(i):
        arrive(2 * i + 1 - core)

    attend(anc_ref, q_ref, own_ref, bias_ref, far_ref, kv_all, k_cat, v_cat, att_ref)
    w_copy.wait()
    width = w_ref.shape[1]
    tile = math.gcd(width, 512)

    @pl.loop(0, width // tile)
    def _(i):
        cols = pl.ds(pl.multiple_of(i * tile, tile), tile)
        proj_ref[:, cols] = jnp.dot(
            att_ref[...], w_vmem[:, cols], preferred_element_type=jnp.float32
        )

    mine.wait()

    @pl.loop(1, lead)
    def _(l):
        kv_copy(me, z_send.at[l], ((z + l) % lead) * 8 + low).wait_send()

    @pl.loop(0, lead)
    def _(l):
        base = ((z + l) % lead) * 8
        for hop in (0, 1, 2):
            kv_copy(base + low, f_send.at[hop, base + low], peers[hop]).wait_send()
        two = base + peers[0] % 8
        for hop in (1, 2):
            kv_copy(two, f_send.at[hop, two], peers[hop]).wait_send()
        for far in (base + across % 8, base + across2 % 8):
            kv_copy(far, f_send.at[2, far], peers[2]).wait_send()

    @pl.loop(1, n)
    def _(d):
        hidden_copy(d).wait_send()
        source = (me + d) % n
        pltpu.make_async_remote_copy(
            src_ref=out_ref.at[source],
            dst_ref=arrived_ref.at[source],
            send_sem=h_send.at[d],
            recv_sem=h_recv.at[source],
            device_id={"ctx": source},
        ).wait_recv()


def on_device(hidden_in, route, queries, keys_values, ancestors, segments, w_out, w_score):
    tok_rows = hidden_in.shape[0]
    half_width = hidden_in.shape[1]
    n = lax.axis_size("ctx")
    capacity = (tok_rows + n - 1) // n + 1
    slot_count = n * capacity
    dest_shard = route // tok_rows
    earlier = jnp.arange(tok_rows)[:, None] > jnp.arange(tok_rows)[None, :]
    same = dest_shard[:, None] == dest_shard[None, :]
    slot_rank = jnp.sum((earlier & same).astype(jnp.int32), axis=1)
    slot_index = dest_shard * capacity + slot_rank
    slot_match = jnp.arange(slot_count, dtype=jnp.int32)[:, None] == slot_index[None, :]
    vacant = jnp.where(jnp.any(slot_match, axis=1), 0.0, EMPTY)
    outgoing = (
        jnp.dot(slot_match.astype(jnp.bfloat16), hidden_in, preferred_element_type=jnp.float32)
        + vacant[:, None]
    ).astype(jnp.bfloat16)
    lines = capacity * half_width // 128
    outgoing = outgoing.reshape(n, lines, 128)

    position = jnp.arange(tok_rows)
    own_mask = (position[None, :] <= position[:, None]) & (segments[None, :] == segments[:, None])
    bias = jnp.where(own_mask, 0.0, neg_big).astype(jnp.float32)
    far_bias = jnp.repeat(jnp.where(ancestors >= 0, 0.0, neg_big), BLOCK, axis=1)
    far_bias = far_bias.astype(jnp.float32)
    key_count = (1 + ancestors.shape[1]) * BLOCK
    vmem = pl.BlockSpec(memory_space=pltpu.VMEM)
    anywhere = pl.BlockSpec(memory_space=pl.ANY)
    dma = pltpu.SemaphoreType.DMA
    arrived, partial_proj = pl.pallas_call(
        functools.partial(kernel, n),
        out_shape=(
            jax.ShapeDtypeStruct((n, lines, 128), jnp.bfloat16),
            jax.ShapeDtypeStruct((tok_rows, w_out.shape[1]), jnp.float32),
        ),
        in_specs=[pl.BlockSpec(memory_space=pltpu.SMEM)] + [vmem] * 4 + [anywhere] * 2,
        out_specs=(anywhere, vmem),
        scratch_shapes=[
            pltpu.VMEM((n, BLOCK, 2 * HEAD), jnp.bfloat16),
            pltpu.VMEM((key_count, HEAD), jnp.bfloat16),
            pltpu.VMEM((key_count, HEAD), jnp.bfloat16),
            pltpu.VMEM(queries.shape, jnp.bfloat16),
            pltpu.VMEM(w_out.shape, jnp.bfloat16),
            dma,
            dma,
            dma((n,)),
            dma((n,)),
            dma((n // 8,)),
            dma((3, n)),
            dma((n,)),
        ],
        compiler_params=pltpu.CompilerParams(
            collective_id=0, has_side_effects=True, vmem_limit_bytes=48 * 1024 * 1024
        ),
    )(ancestors, queries, keys_values, bias, far_bias, outgoing, w_out)

    rows_in = arrived.reshape(slot_count, half_width)
    held = arrived[:, :: half_width // 128, 0].reshape(slot_count) < 0.5 * EMPTY
    before = jnp.arange(slot_count)[None, :] <= jnp.arange(slot_count)[:, None]
    local_slot = jnp.sum((before & held[None, :]).astype(jnp.int32), axis=1) - 1
    local_slot = jnp.where(held, local_slot, -1)
    place_match = (jnp.arange(tok_rows, dtype=jnp.int32)[:, None] == local_slot[None, :]).astype(
        jnp.bfloat16
    )
    hidden_ctx = jnp.dot(place_match, rows_in, preferred_element_type=jnp.float32)
    projected = partial_proj
    if lax.axis_size("tp") > 1:
        projected = lax.psum_scatter(partial_proj, "tp", scatter_dimension=1, tiled=True)
    hidden_out = (hidden_ctx + projected).astype(jnp.bfloat16)
    score_part = jnp.sum(hidden_out.astype(jnp.float32) * w_score[None, :], axis=1)
    token_scores = lax.psum(score_part, "tp")
    return (hidden_out, token_scores)


def solution(mesh):
    placed = (
        P(("group", "ctx"), "tp"),
        P(("group", "ctx")),
        P(("group", "ctx"), "tp"),
        P(("group", "ctx"), None),
        P(("group", "ctx"), None),
        P(("group", "ctx")),
        P("tp", None),
        P("tp"),
    )
    return jax.shard_map(
        on_device,
        mesh=mesh,
        in_specs=placed,
        out_specs=(P(("group", "ctx"), "tp"), P(("group", "ctx"))),
        check_vma=False,
    )
```

```python
import functools
import math

import jax
import jax.numpy as jnp
from jax import lax
from jax.experimental import pallas as pl
from jax.experimental.pallas import tpu as pltpu
from jax.sharding import PartitionSpec as P

HEAD = 128
BLOCK = 128
EMPTY = 64.0


neg_big = -1e30


def partner(me, stride):
    return me + stride * (1 - 2 * ((me // stride) % 2))


def upright(row):
    return jnp.transpose(jnp.broadcast_to(row, (row.shape[1], row.shape[1])))


def iota(shape, axis):
    return lax.broadcasted_iota(jnp.int32, shape, axis)


def pack(n, capacity, route_ref, hid, spread, out_v):
    rows, width = hid.shape
    chunks = width // 128
    slots = n * capacity
    dest = (route_ref[...] // rows).astype(jnp.float32)
    square = (rows, rows)
    ahead = (upright(dest) == dest) & (iota(square, 0) < iota(square, 1))
    rank = jnp.sum(jnp.where(ahead, 1.0, 0.0), axis=0, keepdims=True)
    slot = (dest * capacity + rank).astype(jnp.int32)
    match = jnp.where(iota((slots, rows), 0) == slot, 1.0, 0.0)
    vacant = EMPTY * (1.0 - jnp.sum(match, axis=1, keepdims=True))
    match = match.astype(jnp.bfloat16)
    for first in range(0, chunks, 4):
        many = min(4, chunks - first)
        part = hid[:, first * 128 : (first + many) * 128]
        part = jnp.dot(match, part, preferred_element_type=jnp.float32) + vacant
        for c in range(many):
            spread[pl.ds(first + c, slots, stride=chunks), :] = part[:, c * 128 : (c + 1) * 128]
    lines = capacity * chunks

    @pl.loop(0, n)
    def _(i):
        out_v[i] = spread[pl.ds(pl.multiple_of(i * lines, lines), lines), :].astype(jnp.bfloat16)


def placement(slots, rows, first):
    held = jnp.where(first < 0.5 * EMPTY, 1.0, 0.0).astype(jnp.bfloat16)
    shape = (slots, slots)
    upper = jnp.where(iota(shape, 0) <= iota(shape, 1), 1.0, 0.0).astype(jnp.bfloat16)
    unit = jnp.where(iota(shape, 0) == iota(shape, 1), 1.0, 0.0).astype(jnp.bfloat16)
    turned = (((0,), (0,)), ((), ()))
    count = lax.dot_general(held, upper, turned, preferred_element_type=jnp.float32)
    here = lax.dot_general(held, unit, turned, preferred_element_type=jnp.float32)
    spot = iota((rows, slots), 0).astype(jnp.float32) + 1.0
    return jnp.where(count == spot, here, 0.0).astype(jnp.bfloat16)


def attend(anc_ref, q_ref, own_ref, seg_ref, kv_all, k_cat, v_cat, att_ref):
    seg = seg_ref[...].astype(jnp.float32)
    square = (BLOCK, BLOCK)
    own_mask = (upright(seg) == seg) & (iota(square, 1) <= iota(square, 0))
    near_bias = jnp.where(own_mask, 0.0, neg_big)
    far_bias = jnp.concatenate(
        [
            jnp.full((1, BLOCK), jnp.where(anc_ref[0, j] >= 0, 0.0, neg_big), jnp.float32)
            for j in range(anc_ref.shape[1])
        ],
        axis=1,
    )
    listed = anc_ref.shape[1]
    k_cat[0:BLOCK, :] = own_ref[:, :HEAD]
    v_cat[0:BLOCK, :] = own_ref[:, HEAD:]
    for j in range(listed):
        block = kv_all[jnp.maximum(anc_ref[0, j], 0)]
        rows = slice((j + 1) * BLOCK, (j + 2) * BLOCK)
        k_cat[rows, :] = block[:, :HEAD]
        v_cat[rows, :] = block[:, HEAD:]
    scale = 1.0 / math.sqrt(HEAD)
    for h in range(q_ref.shape[1] // HEAD):
        cols = slice(h * HEAD, (h + 1) * HEAD)
        logits = lax.dot_general(
            q_ref[:, cols],
            k_cat[...],
            (((1,), (1,)), ((), ())),
            preferred_element_type=jnp.float32,
        )
        near = logits[:, :BLOCK] * scale + near_bias
        far = logits[:, BLOCK:] * scale + far_bias
        logits = jnp.concatenate([near, far], axis=1)
        top = jnp.max(logits, axis=1, keepdims=True)
        terms = jnp.exp(logits - top)
        total = jnp.sum(terms, axis=1, keepdims=True)
        weighted = jnp.dot(
            terms.astype(jnp.bfloat16), v_cat[...], preferred_element_type=jnp.float32
        )
        att_ref[:, cols] = (weighted / total).astype(jnp.bfloat16)


def kernel(
    n,
    capacity,
    finish,
    anc_ref,
    q_ref,
    own_ref,
    route_ref,
    seg_ref,
    score_w_ref,
    hid_ref,
    w_ref,
    hidden_ref,
    second_ref,
    out_ref,
    arrived_ref,
    spread,
    landed,
    hid,
    proj_v,
    kv_all,
    k_cat,
    v_cat,
    att_ref,
    w_vmem,
    w_sem,
    hid_sem,
    h_send,
    h_recv,
    z_send,
    f_send,
    kv_recv,
):
    me = lax.axis_index("ctx")
    lead = n // 8
    low = me % 8
    z = me // 8
    core = me % 2
    stride2 = 4 - 2 * core
    stride3 = 2 + 2 * core
    peers = (partner(me, stride2), partner(me, stride3), partner(me, 1))

    w_copy = pltpu.make_async_copy(w_ref, w_vmem, w_sem)
    w_copy.start()
    hid_copy = pltpu.make_async_copy(hid_ref, hid, hid_sem)
    hid_copy.start()
    kv_all[me] = own_ref[...]

    barrier = pltpu.get_barrier_semaphore()

    @pl.loop(1, n)
    def _(d):
        pl.semaphore_signal(barrier, inc=1, device_id={"ctx": (me + d) % n})

    pl.semaphore_wait(barrier, n - 1)

    def shift(d):
        return (d * 11) % n

    def hidden_copy(d):
        to = (me + shift(d)) % n
        return pltpu.make_async_remote_copy(
            src_ref=out_ref.at[to],
            dst_ref=arrived_ref.at[me],
            send_sem=h_send.at[d],
            recv_sem=h_recv.at[me],
            device_id={"ctx": to},
        )

    def send_hidden(first, count):
        @pl.loop(0, count)
        def _(i):
            hidden_copy(first + i).start()

    def kv_copy(block, send_sem, to):
        return pltpu.make_async_remote_copy(
            src_ref=kv_all.at[block],
            dst_ref=kv_all.at[block],
            send_sem=send_sem,
            recv_sem=kv_recv.at[block],
            device_id={"ctx": to},
        )

    def arrive(block):
        kv_copy(block, z_send.at[0], peers[2]).wait_recv()

    def forward(block, hops):
        for hop in hops:
            kv_copy(block, f_send.at[hop, block], peers[hop]).start()

    @pl.loop(1, lead)
    def _(l):
        kv_copy(me, z_send.at[l], ((z + l) % lead) * 8 + low).start()

    forward(me, (0, 1, 2))

    total = n - 1
    at_start = total // 4
    each = (total - at_start) // (2 * lead)
    second = 1 + at_start + each * (lead - 1)
    third = second + each * lead
    hid_copy.wait()
    pack(n, capacity, route_ref, hid, spread, out_ref)
    send_hidden(1, at_start)

    @pl.loop(1, lead)
    def _(l):
        block = ((z + l) % lead) * 8 + low
        arrive(block)
        forward(block, (0, 1, 2))
        send_hidden(1 + at_start + each * (l - 1), each)

    @pl.loop(0, lead)
    def _(l):
        block = ((z + l) % lead) * 8 + peers[0] % 8
        arrive(block)
        forward(block, (1, 2))
        send_hidden(second + each * l, each)

    send_hidden(third, n - third)
    across = peers[1]

    @pl.loop(0, lead)
    def _(l):
        block = ((z + l) % lead) * 8 + across % 8
        arrive(block)
        forward(block, (2,))

    across2 = partner(across, stride2)

    @pl.loop(0, lead)
    def _(l):
        block = ((z + l) % lead) * 8 + across2 % 8
        arrive(block)
        forward(block, (2,))

    @pl.loop(0, n // 2)
    def _(i):
        arrive(2 * i + 1 - core)

    attend(anc_ref, q_ref, own_ref, seg_ref, kv_all, k_cat, v_cat, att_ref)
    w_copy.wait()
    width = w_ref.shape[1]
    tile = math.gcd(width, 512)
    proj_to = proj_v if finish else second_ref

    @pl.loop(0, width // tile)
    def _(i):
        cols = pl.ds(pl.multiple_of(i * tile, tile), tile)
        proj_to[:, cols] = jnp.dot(
            att_ref[...], w_vmem[:, cols], preferred_element_type=jnp.float32
        )

    @pl.loop(1, lead)
    def _(l):
        kv_copy(me, z_send.at[l], ((z + l) % lead) * 8 + low).wait_send()

    @pl.loop(0, lead)
    def _(l):
        base = ((z + l) % lead) * 8
        for hop in (0, 1, 2):
            kv_copy(base + low, f_send.at[hop, base + low], peers[hop]).wait_send()
        two = base + peers[0] % 8
        for hop in (1, 2):
            kv_copy(two, f_send.at[hop, two], peers[hop]).wait_send()
        for far in (base + across % 8, base + across2 % 8):
            kv_copy(far, f_send.at[2, far], peers[2]).wait_send()

    lines = out_ref.shape[1]
    own_lines = pl.ds(pl.multiple_of(me * lines, lines), lines)
    landed[own_lines, :] = spread[own_lines, :]

    @pl.loop(1, n)
    def _(d):
        source = (me + n - shift(d)) % n
        pltpu.make_async_remote_copy(
            src_ref=out_ref.at[source],
            dst_ref=arrived_ref.at[source],
            send_sem=h_send.at[d],
            recv_sem=h_recv.at[source],
            device_id={"ctx": source},
        ).wait_recv()
        landed[pl.ds(pl.multiple_of(source * lines, lines), lines), :] = arrived_ref[
            source
        ].astype(jnp.float32)

    rows, held_width = hid.shape
    chunks = held_width // 128
    slots = n * capacity

    def column(c):
        return landed[pl.ds(c, slots, stride=chunks), :]

    place = placement(slots, rows, column(0))
    tally = jnp.zeros((rows, 128), jnp.float32)
    for first in range(0, chunks, 2):
        many = min(2, chunks - first)
        part = jnp.concatenate([column(first + c) for c in range(many)], axis=1)
        part = jnp.dot(place, part.astype(jnp.bfloat16), preferred_element_type=jnp.float32)
        cols = slice(first * 128, (first + many) * 128)
        if finish:
            part = (part + proj_v[:, cols]).astype(jnp.bfloat16)
            scored = part.astype(jnp.float32) * score_w_ref[:, cols]
            for c in range(many):
                tally = tally + scored[:, c * 128 : (c + 1) * 128]
        hidden_ref[:, cols] = part.astype(jnp.bfloat16)
    if finish:
        second_ref[...] = jnp.sum(jnp.transpose(tally), axis=0, keepdims=True)

    @pl.loop(1, n)
    def _(d):
        hidden_copy(d).wait_send()


def on_device(hidden_in, route, queries, keys_values, ancestors, segments, w_out, w_score):
    tok_rows = hidden_in.shape[0]
    half_width = hidden_in.shape[1]
    n = lax.axis_size("ctx")
    capacity = (tok_rows + n - 1) // n + 1
    finish = lax.axis_size("tp") == 1
    lines = capacity * half_width // 128
    key_count = (1 + ancestors.shape[1]) * BLOCK
    vmem = pl.BlockSpec(memory_space=pltpu.VMEM)
    anywhere = pl.BlockSpec(memory_space=pl.ANY)
    dma = pltpu.SemaphoreType.DMA
    wide = (tok_rows, w_out.shape[1])
    hidden, second = pl.pallas_call(
        functools.partial(kernel, n, capacity, finish),
        out_shape=(
            jax.ShapeDtypeStruct((tok_rows, half_width), jnp.bfloat16),
            jax.ShapeDtypeStruct((1, tok_rows) if finish else wide, jnp.float32),
        ),
        in_specs=[pl.BlockSpec(memory_space=pltpu.SMEM)] + [vmem] * 5 + [anywhere] * 2,
        out_specs=(vmem, vmem),
        scratch_shapes=[
            pltpu.VMEM((n, lines, 128), jnp.bfloat16),
            pltpu.VMEM((n, lines, 128), jnp.bfloat16),
            pltpu.VMEM((n * lines, 128), jnp.float32),
            pltpu.VMEM((n * lines, 128), jnp.float32),
            pltpu.VMEM(hidden_in.shape, jnp.bfloat16),
            pltpu.VMEM(wide if finish else (8, 128), jnp.float32),
            pltpu.VMEM((n, BLOCK, 2 * HEAD), jnp.bfloat16),
            pltpu.VMEM((key_count, HEAD), jnp.bfloat16),
            pltpu.VMEM((key_count, HEAD), jnp.bfloat16),
            pltpu.VMEM(queries.shape, jnp.bfloat16),
            pltpu.VMEM(w_out.shape, jnp.bfloat16),
            dma,
            dma,
            dma((n,)),
            dma((n,)),
            dma((n // 8,)),
            dma((3, n)),
            dma((n,)),
        ],
        compiler_params=pltpu.CompilerParams(
            collective_id=0, has_side_effects=True, vmem_limit_bytes=48 * 1024 * 1024
        ),
    )(
        ancestors,
        queries,
        keys_values,
        route.reshape(1, tok_rows),
        segments.reshape(1, tok_rows),
        w_score.reshape(1, w_score.shape[0]),
        hidden_in,
        w_out,
    )
    if finish:
        return (hidden, second.reshape(tok_rows))
    projected = lax.psum_scatter(second, "tp", scatter_dimension=1, tiled=True)
    hidden_out = (hidden.astype(jnp.float32) + projected).astype(jnp.bfloat16)
    score_part = jnp.sum(hidden_out.astype(jnp.float32) * w_score[None, :], axis=1)
    return (hidden_out, lax.psum(score_part, "tp"))


def solution(mesh):
    placed = (
        P(("group", "ctx"), "tp"),
        P(("group", "ctx")),
        P(("group", "ctx"), "tp"),
        P(("group", "ctx"), None),
        P(("group", "ctx"), None),
        P(("group", "ctx")),
        P("tp", None),
        P("tp"),
    )
    return jax.shard_map(
        on_device,
        mesh=mesh,
        in_specs=placed,
        out_specs=(P(("group", "ctx"), "tp"), P(("group", "ctx"))),
        check_vma=False,
    )
```

```python
import functools
import math

import jax
import jax.numpy as jnp
from jax import lax
from jax.experimental import pallas as pl
from jax.experimental.pallas import tpu as pltpu
from jax.sharding import PartitionSpec as P

HEAD = 128
BLOCK = 128
EMPTY = 64.0


neg_big = -1e30


def partner(me, stride):
    return me + stride * (1 - 2 * ((me // stride) % 2))


def upright(row):
    return jnp.transpose(jnp.broadcast_to(row, (row.shape[1], row.shape[1])))


def iota(shape, axis):
    return lax.broadcasted_iota(jnp.int32, shape, axis)


def pack(n, capacity, route_ref, hid, spread, out_v):
    rows, width = hid.shape
    chunks = width // 128
    slots = n * capacity
    dest = (route_ref[...] // rows).astype(jnp.float32)
    square = (rows, rows)
    ahead = (upright(dest) == dest) & (iota(square, 0) < iota(square, 1))
    rank = jnp.sum(jnp.where(ahead, 1.0, 0.0), axis=0, keepdims=True)
    slot = (dest * capacity + rank).astype(jnp.int32)
    match = jnp.where(iota((slots, rows), 0) == slot, 1.0, 0.0)
    vacant = EMPTY * (1.0 - jnp.sum(match, axis=1, keepdims=True))
    match = match.astype(jnp.bfloat16)
    for first in range(0, chunks, 4):
        many = min(4, chunks - first)
        part = hid[:, first * 128 : (first + many) * 128]
        part = jnp.dot(match, part, preferred_element_type=jnp.float32) + vacant
        for c in range(many):
            spread[pl.ds(first + c, slots, stride=chunks), :] = part[:, c * 128 : (c + 1) * 128]
    lines = capacity * chunks

    @pl.loop(0, n)
    def _(i):
        out_v[i] = spread[pl.ds(pl.multiple_of(i * lines, lines), lines), :].astype(jnp.bfloat16)


def placement(slots, rows, first):
    held = jnp.where(first < 0.5 * EMPTY, 1.0, 0.0).astype(jnp.bfloat16)
    shape = (slots, slots)
    upper = jnp.where(iota(shape, 0) <= iota(shape, 1), 1.0, 0.0).astype(jnp.bfloat16)
    unit = jnp.where(iota(shape, 0) == iota(shape, 1), 1.0, 0.0).astype(jnp.bfloat16)
    turned = (((0,), (0,)), ((), ()))
    count = lax.dot_general(held, upper, turned, preferred_element_type=jnp.float32)
    here = lax.dot_general(held, unit, turned, preferred_element_type=jnp.float32)
    spot = iota((rows, slots), 0).astype(jnp.float32) + 1.0
    return jnp.where(count == spot, here, 0.0).astype(jnp.bfloat16)


def attend(anc_ref, q_ref, own_ref, seg_ref, kv_all, k_cat, v_cat, att_ref):
    seg = seg_ref[...].astype(jnp.float32)
    square = (BLOCK, BLOCK)
    own_mask = (upright(seg) == seg) & (iota(square, 1) <= iota(square, 0))
    near_bias = jnp.where(own_mask, 0.0, neg_big)
    far_bias = jnp.concatenate(
        [
            jnp.full((1, BLOCK), jnp.where(anc_ref[0, j] >= 0, 0.0, neg_big), jnp.float32)
            for j in range(anc_ref.shape[1])
        ],
        axis=1,
    )
    listed = anc_ref.shape[1]
    k_cat[0:BLOCK, :] = own_ref[:, :HEAD]
    v_cat[0:BLOCK, :] = own_ref[:, HEAD:]
    for j in range(listed):
        block = kv_all[jnp.maximum(anc_ref[0, j], 0)]
        rows = slice((j + 1) * BLOCK, (j + 2) * BLOCK)
        k_cat[rows, :] = block[:, :HEAD]
        v_cat[rows, :] = block[:, HEAD:]
    scale = 1.0 / math.sqrt(HEAD)
    for h in range(q_ref.shape[1] // HEAD):
        cols = slice(h * HEAD, (h + 1) * HEAD)
        logits = lax.dot_general(
            q_ref[:, cols],
            k_cat[...],
            (((1,), (1,)), ((), ())),
            preferred_element_type=jnp.float32,
        )
        near = logits[:, :BLOCK] * scale + near_bias
        far = logits[:, BLOCK:] * scale + far_bias
        logits = jnp.concatenate([near, far], axis=1)
        top = jnp.max(logits, axis=1, keepdims=True)
        terms = jnp.exp(logits - top)
        total = jnp.sum(terms, axis=1, keepdims=True)
        weighted = jnp.dot(
            terms.astype(jnp.bfloat16), v_cat[...], preferred_element_type=jnp.float32
        )
        att_ref[:, cols] = (weighted / total).astype(jnp.bfloat16)


def kernel(
    n,
    capacity,
    finish,
    anc_ref,
    q_in,
    own_in,
    route_in,
    seg_in,
    score_w_in,
    hid_in,
    w_ref,
    hidden_ref,
    second_ref,
    out_ref,
    arrived_ref,
    spread,
    landed,
    hid,
    proj_v,
    kv_all,
    k_cat,
    v_cat,
    att_ref,
    w_vmem,
    q_ref,
    own_ref,
    route_ref,
    seg_ref,
    score_w_ref,
    w_sem,
    in_sem,
    h_send,
    h_recv,
    z_send,
    f_send,
    kv_recv,
):
    me = lax.axis_index("ctx")
    lead = n // 8
    low = me % 8
    z = me // 8
    core = me % 2
    stride2 = 4 - 2 * core
    stride3 = 2 + 2 * core
    peers = (partner(me, stride2), partner(me, stride3), partner(me, 1))

    own_copy, route_copy, hid_copy, q_copy, seg_copy, score_copy = [
        pltpu.make_async_copy(source, target, in_sem.at[i])
        for i, (source, target) in enumerate(
            [
                (own_in, own_ref),
                (route_in, route_ref),
                (hid_in, hid),
                (q_in, q_ref),
                (seg_in, seg_ref),
                (score_w_in, score_w_ref),
            ]
        )
    ]
    early = (own_copy, route_copy, hid_copy, q_copy, seg_copy, score_copy)
    for copy in early:
        copy.start()
    w_copy = pltpu.make_async_copy(w_ref, w_vmem, w_sem)
    w_copy.start()

    barrier = pltpu.get_barrier_semaphore()

    @pl.loop(1, n)
    def _(d):
        pl.semaphore_signal(barrier, inc=1, device_id={"ctx": (me + d) % n})

    own_copy.wait()
    kv_all[me] = own_ref[...]
    pl.semaphore_wait(barrier, n - 1)

    def shift(d):
        return (d * 11) % n

    def hidden_copy(d):
        to = (me + shift(d)) % n
        return pltpu.make_async_remote_copy(
            src_ref=out_ref.at[to],
            dst_ref=arrived_ref.at[me],
            send_sem=h_send.at[d],
            recv_sem=h_recv.at[me],
            device_id={"ctx": to},
        )

    def send_hidden(first, count):
        @pl.loop(0, count)
        def _(i):
            hidden_copy(first + i).start()

    def kv_copy(block, send_sem, to):
        return pltpu.make_async_remote_copy(
            src_ref=kv_all.at[block],
            dst_ref=kv_all.at[block],
            send_sem=send_sem,
            recv_sem=kv_recv.at[block],
            device_id={"ctx": to},
        )

    def arrive(block):
        kv_copy(block, z_send.at[0], peers[2]).wait_recv()

    def forward(block, hops):
        for hop in hops:
            kv_copy(block, f_send.at[hop, block], peers[hop]).start()

    @pl.loop(1, lead)
    def _(l):
        kv_copy(me, z_send.at[l], ((z + l) % lead) * 8 + low).start()

    forward(me, (0, 1, 2))

    total = n - 1
    at_start = total // 4
    each = (total - at_start) // (2 * lead)
    second = 1 + at_start + each * (lead - 1)
    third = second + each * lead
    route_copy.wait()
    hid_copy.wait()
    pack(n, capacity, route_ref, hid, spread, out_ref)
    send_hidden(1, at_start)

    @pl.loop(1, lead)
    def _(l):
        block = ((z + l) % lead) * 8 + low
        arrive(block)
        forward(block, (0, 1, 2))
        send_hidden(1 + at_start + each * (l - 1), each)

    @pl.loop(0, lead)
    def _(l):
        block = ((z + l) % lead) * 8 + peers[0] % 8
        arrive(block)
        forward(block, (1, 2))
        send_hidden(second + each * l, each)

    send_hidden(third, n - third)
    across = peers[1]

    @pl.loop(0, lead)
    def _(l):
        block = ((z + l) % lead) * 8 + across % 8
        arrive(block)
        forward(block, (2,))

    across2 = partner(across, stride2)

    @pl.loop(0, lead)
    def _(l):
        block = ((z + l) % lead) * 8 + across2 % 8
        arrive(block)
        forward(block, (2,))

    @pl.loop(0, n // 2)
    def _(i):
        arrive(2 * i + 1 - core)

    q_copy.wait()
    seg_copy.wait()
    attend(anc_ref, q_ref, own_ref, seg_ref, kv_all, k_cat, v_cat, att_ref)
    w_copy.wait()
    width = w_ref.shape[1]
    tile = math.gcd(width, 512)
    proj_to = proj_v if finish else second_ref

    @pl.loop(0, width // tile)
    def _(i):
        cols = pl.ds(pl.multiple_of(i * tile, tile), tile)
        proj_to[:, cols] = jnp.dot(
            att_ref[...], w_vmem[:, cols], preferred_element_type=jnp.float32
        )

    @pl.loop(1, lead)
    def _(l):
        kv_copy(me, z_send.at[l], ((z + l) % lead) * 8 + low).wait_send()

    @pl.loop(0, lead)
    def _(l):
        base = ((z + l) % lead) * 8
        for hop in (0, 1, 2):
            kv_copy(base + low, f_send.at[hop, base + low], peers[hop]).wait_send()
        two = base + peers[0] % 8
        for hop in (1, 2):
            kv_copy(two, f_send.at[hop, two], peers[hop]).wait_send()
        for far in (base + across % 8, base + across2 % 8):
            kv_copy(far, f_send.at[2, far], peers[2]).wait_send()

    lines = out_ref.shape[1]
    own_lines = pl.ds(pl.multiple_of(me * lines, lines), lines)
    landed[own_lines, :] = spread[own_lines, :]

    @pl.loop(1, n)
    def _(d):
        source = (me + n - shift(d)) % n
        pltpu.make_async_remote_copy(
            src_ref=out_ref.at[source],
            dst_ref=arrived_ref.at[source],
            send_sem=h_send.at[d],
            recv_sem=h_recv.at[source],
            device_id={"ctx": source},
        ).wait_recv()
        landed[pl.ds(pl.multiple_of(source * lines, lines), lines), :] = arrived_ref[
            source
        ].astype(jnp.float32)

    score_copy.wait()
    rows, held_width = hid.shape
    chunks = held_width // 128
    slots = n * capacity

    def column(c):
        return landed[pl.ds(c, slots, stride=chunks), :]

    place = placement(slots, rows, column(0))
    tally = jnp.zeros((rows, 128), jnp.float32)
    for first in range(0, chunks, 2):
        many = min(2, chunks - first)
        part = jnp.concatenate([column(first + c) for c in range(many)], axis=1)
        part = jnp.dot(place, part.astype(jnp.bfloat16), preferred_element_type=jnp.float32)
        cols = slice(first * 128, (first + many) * 128)
        if finish:
            part = (part + proj_v[:, cols]).astype(jnp.bfloat16)
            scored = part.astype(jnp.float32) * score_w_ref[:, cols]
            for c in range(many):
                tally = tally + scored[:, c * 128 : (c + 1) * 128]
        hidden_ref[:, cols] = part.astype(jnp.bfloat16)
    if finish:
        second_ref[...] = jnp.sum(jnp.transpose(tally), axis=0, keepdims=True)

    @pl.loop(1, n)
    def _(d):
        hidden_copy(d).wait_send()


def on_device(hidden_in, route, queries, keys_values, ancestors, segments, w_out, w_score):
    tok_rows = hidden_in.shape[0]
    half_width = hidden_in.shape[1]
    n = lax.axis_size("ctx")
    capacity = (tok_rows + n - 1) // n + 1
    finish = lax.axis_size("tp") == 1
    lines = capacity * half_width // 128
    key_count = (1 + ancestors.shape[1]) * BLOCK
    vmem = pl.BlockSpec(memory_space=pltpu.VMEM)
    anywhere = pl.BlockSpec(memory_space=pl.ANY)
    dma = pltpu.SemaphoreType.DMA
    wide = (tok_rows, w_out.shape[1])
    hidden, second = pl.pallas_call(
        functools.partial(kernel, n, capacity, finish),
        out_shape=(
            jax.ShapeDtypeStruct((tok_rows, half_width), jnp.bfloat16),
            jax.ShapeDtypeStruct((1, tok_rows) if finish else wide, jnp.float32),
        ),
        in_specs=[pl.BlockSpec(memory_space=pltpu.SMEM)] + [anywhere] * 7,
        out_specs=(vmem, vmem),
        scratch_shapes=[
            pltpu.VMEM((n, lines, 128), jnp.bfloat16),
            pltpu.VMEM((n, lines, 128), jnp.bfloat16),
            pltpu.VMEM((n * lines, 128), jnp.float32),
            pltpu.VMEM((n * lines, 128), jnp.float32),
            pltpu.VMEM(hidden_in.shape, jnp.bfloat16),
            pltpu.VMEM(wide if finish else (8, 128), jnp.float32),
            pltpu.VMEM((n, BLOCK, 2 * HEAD), jnp.bfloat16),
            pltpu.VMEM((key_count, HEAD), jnp.bfloat16),
            pltpu.VMEM((key_count, HEAD), jnp.bfloat16),
            pltpu.VMEM(queries.shape, jnp.bfloat16),
            pltpu.VMEM(w_out.shape, jnp.bfloat16),
            pltpu.VMEM(queries.shape, jnp.bfloat16),
            pltpu.VMEM(keys_values.shape, jnp.bfloat16),
            pltpu.VMEM((1, tok_rows), jnp.int32),
            pltpu.VMEM((1, tok_rows), jnp.int32),
            pltpu.VMEM((1, w_score.shape[0]), jnp.float32),
            dma,
            dma((6,)),
            dma((n,)),
            dma((n,)),
            dma((n // 8,)),
            dma((3, n)),
            dma((n,)),
        ],
        compiler_params=pltpu.CompilerParams(
            collective_id=0, has_side_effects=True, vmem_limit_bytes=60 * 1024 * 1024
        ),
    )(
        ancestors,
        queries,
        keys_values,
        route.reshape(1, tok_rows),
        segments.reshape(1, tok_rows),
        w_score.reshape(1, w_score.shape[0]),
        hidden_in,
        w_out,
    )
    if finish:
        return (hidden, second.reshape(tok_rows))
    projected = lax.psum_scatter(second, "tp", scatter_dimension=1, tiled=True)
    hidden_out = (hidden.astype(jnp.float32) + projected).astype(jnp.bfloat16)
    score_part = jnp.sum(hidden_out.astype(jnp.float32) * w_score[None, :], axis=1)
    return (hidden_out, lax.psum(score_part, "tp"))


def solution(mesh):
    placed = (
        P(("group", "ctx"), "tp"),
        P(("group", "ctx")),
        P(("group", "ctx"), "tp"),
        P(("group", "ctx"), None),
        P(("group", "ctx"), None),
        P(("group", "ctx")),
        P("tp", None),
        P("tp"),
    )
    return jax.shard_map(
        on_device,
        mesh=mesh,
        in_specs=placed,
        out_specs=(P(("group", "ctx"), "tp"), P(("group", "ctx"))),
        check_vma=False,
    )
```

```python
import functools
import math

import jax
import jax.numpy as jnp
from jax import lax
from jax.experimental import pallas as pl
from jax.experimental.pallas import tpu as pltpu
from jax.sharding import PartitionSpec as P

HEAD = 128
BLOCK = 128
EMPTY = 64.0


neg_big = -1e30


def partner(me, stride):
    return me + stride * (1 - 2 * ((me // stride) % 2))


def upright(row):
    return jnp.transpose(jnp.broadcast_to(row, (row.shape[1], row.shape[1])))


def iota(shape, axis):
    return lax.broadcasted_iota(jnp.int32, shape, axis)


def pack(n, capacity, route_ref, hid, spread, out_v):
    rows, width = hid.shape
    chunks = width // 128
    slots = n * capacity
    dest = (route_ref[...] // rows).astype(jnp.float32)
    square = (rows, rows)
    ahead = (upright(dest) == dest) & (iota(square, 0) < iota(square, 1))
    rank = jnp.sum(jnp.where(ahead, 1.0, 0.0), axis=0, keepdims=True)
    slot = (dest * capacity + rank).astype(jnp.int32)
    match = jnp.where(iota((slots, rows), 0) == slot, 1.0, 0.0)
    vacant = EMPTY * (1.0 - jnp.sum(match, axis=1, keepdims=True))
    match = match.astype(jnp.bfloat16)
    for first in range(0, chunks, 4):
        many = min(4, chunks - first)
        part = hid[:, first * 128 : (first + many) * 128]
        part = jnp.dot(match, part, preferred_element_type=jnp.float32) + vacant
        for c in range(many):
            spread[pl.ds(first + c, slots, stride=chunks), :] = part[:, c * 128 : (c + 1) * 128]
    lines = capacity * chunks

    @pl.loop(0, n)
    def _(i):
        out_v[i] = spread[pl.ds(pl.multiple_of(i * lines, lines), lines), :].astype(jnp.bfloat16)


def placement(slots, rows, first):
    held = jnp.where(first < 0.5 * EMPTY, 1.0, 0.0).astype(jnp.bfloat16)
    shape = (slots, slots)
    upper = jnp.where(iota(shape, 0) <= iota(shape, 1), 1.0, 0.0).astype(jnp.bfloat16)
    unit = jnp.where(iota(shape, 0) == iota(shape, 1), 1.0, 0.0).astype(jnp.bfloat16)
    turned = (((0,), (0,)), ((), ()))
    count = lax.dot_general(held, upper, turned, preferred_element_type=jnp.float32)
    here = lax.dot_general(held, unit, turned, preferred_element_type=jnp.float32)
    spot = iota((rows, slots), 0).astype(jnp.float32) + 1.0
    return jnp.where(count == spot, here, 0.0).astype(jnp.bfloat16)


def attend(anc_ref, q_ref, own_ref, seg_ref, kv_all, k_cat, v_cat, att_ref):
    seg = seg_ref[...].astype(jnp.float32)
    square = (BLOCK, BLOCK)
    own_mask = (upright(seg) == seg) & (iota(square, 1) <= iota(square, 0))
    near_bias = jnp.where(own_mask, 0.0, neg_big)
    far_bias = jnp.concatenate(
        [
            jnp.full((1, BLOCK), jnp.where(anc_ref[0, j] >= 0, 0.0, neg_big), jnp.float32)
            for j in range(anc_ref.shape[1])
        ],
        axis=1,
    )
    listed = anc_ref.shape[1]
    k_cat[0:BLOCK, :] = own_ref[:, :HEAD]
    v_cat[0:BLOCK, :] = own_ref[:, HEAD:]
    for j in range(listed):
        block = kv_all[jnp.maximum(anc_ref[0, j], 0)]
        rows = slice((j + 1) * BLOCK, (j + 2) * BLOCK)
        k_cat[rows, :] = block[:, :HEAD]
        v_cat[rows, :] = block[:, HEAD:]
    scale = 1.0 / math.sqrt(HEAD)
    for h in range(q_ref.shape[1] // HEAD):
        cols = slice(h * HEAD, (h + 1) * HEAD)
        logits = lax.dot_general(
            q_ref[:, cols],
            k_cat[...],
            (((1,), (1,)), ((), ())),
            preferred_element_type=jnp.float32,
        )
        near = logits[:, :BLOCK] * scale + near_bias
        far = logits[:, BLOCK:] * scale + far_bias
        logits = jnp.concatenate([near, far], axis=1)
        top = jnp.max(logits, axis=1, keepdims=True)
        terms = jnp.exp(logits - top)
        total = jnp.sum(terms, axis=1, keepdims=True)
        weighted = jnp.dot(
            terms.astype(jnp.bfloat16), v_cat[...], preferred_element_type=jnp.float32
        )
        att_ref[:, cols] = (weighted / total).astype(jnp.bfloat16)


def kernel(
    n,
    capacity,
    finish,
    anc_ref,
    q_in,
    own_in,
    route_in,
    seg_in,
    score_w_in,
    hid_in,
    w_ref,
    hidden_ref,
    second_ref,
    out_ref,
    arrived_ref,
    spread,
    landed,
    hid,
    proj_v,
    kv_all,
    k_cat,
    v_cat,
    att_ref,
    w_vmem,
    q_ref,
    own_ref,
    route_ref,
    seg_ref,
    score_w_ref,
    w_sem,
    in_sem,
    h_send,
    h_recv,
    z_send,
    f_send,
    kv_recv,
):
    me = lax.axis_index("ctx")
    lead = n // 8
    low = me % 8
    z = me // 8
    core = me % 2
    stride2 = 4 - 2 * core
    stride3 = 2 + 2 * core
    peers = (partner(me, stride2), partner(me, stride3), partner(me, 1))

    own_copy, route_copy, hid_copy, q_copy, seg_copy, score_copy = [
        pltpu.make_async_copy(source, target, in_sem.at[i])
        for i, (source, target) in enumerate(
            [
                (own_in, own_ref),
                (route_in, route_ref),
                (hid_in, hid),
                (q_in, q_ref),
                (seg_in, seg_ref),
                (score_w_in, score_w_ref),
            ]
        )
    ]
    early = (own_copy, route_copy, hid_copy, q_copy, seg_copy, score_copy)
    for copy in early:
        copy.start()
    w_copy = pltpu.make_async_copy(w_ref, w_vmem, w_sem)
    w_copy.start()

    barrier = pltpu.get_barrier_semaphore()

    @pl.loop(1, n)
    def _(d):
        pl.semaphore_signal(barrier, inc=1, device_id={"ctx": (me + d) % n})

    own_copy.wait()
    kv_all[me] = own_ref[...]
    pl.semaphore_wait(barrier, n - 1)

    def shift(d):
        return (d * 5) % n

    def hidden_copy(d):
        to = (me + shift(d)) % n
        return pltpu.make_async_remote_copy(
            src_ref=out_ref.at[to],
            dst_ref=arrived_ref.at[me],
            send_sem=h_send.at[d],
            recv_sem=h_recv.at[me],
            device_id={"ctx": to},
        )

    def send_hidden(first, count):
        @pl.loop(0, count)
        def _(i):
            hidden_copy(first + i).start()

    def kv_copy(block, send_sem, to):
        return pltpu.make_async_remote_copy(
            src_ref=kv_all.at[block],
            dst_ref=kv_all.at[block],
            send_sem=send_sem,
            recv_sem=kv_recv.at[block],
            device_id={"ctx": to},
        )

    def arrive(block):
        kv_copy(block, z_send.at[0], peers[2]).wait_recv()

    def forward(block, hops):
        for hop in hops:
            kv_copy(block, f_send.at[hop, block], peers[hop]).start()

    @pl.loop(1, lead)
    def _(l):
        kv_copy(me, z_send.at[l], ((z + l) % lead) * 8 + low).start()

    forward(me, (0, 1, 2))

    total = n - 1
    at_start = total // 4
    each = (total - at_start) // (2 * lead)
    second = 1 + at_start + each * (lead - 1)
    third = second + each * lead
    route_copy.wait()
    hid_copy.wait()
    pack(n, capacity, route_ref, hid, spread, out_ref)
    send_hidden(1, at_start)

    @pl.loop(1, lead)
    def _(l):
        block = ((z + l) % lead) * 8 + low
        arrive(block)
        forward(block, (0, 1, 2))
        send_hidden(1 + at_start + each * (l - 1), each)

    @pl.loop(0, lead)
    def _(l):
        block = ((z + l) % lead) * 8 + peers[0] % 8
        arrive(block)
        forward(block, (1, 2))
        send_hidden(second + each * l, each)

    send_hidden(third, n - third)
    across = peers[1]

    @pl.loop(0, lead)
    def _(l):
        block = ((z + l) % lead) * 8 + across % 8
        arrive(block)
        forward(block, (2,))

    across2 = partner(across, stride2)

    @pl.loop(0, lead)
    def _(l):
        block = ((z + l) % lead) * 8 + across2 % 8
        arrive(block)
        forward(block, (2,))

    @pl.loop(0, n // 2)
    def _(i):
        arrive(2 * i + 1 - core)

    q_copy.wait()
    seg_copy.wait()
    attend(anc_ref, q_ref, own_ref, seg_ref, kv_all, k_cat, v_cat, att_ref)
    w_copy.wait()
    width = w_ref.shape[1]
    tile = math.gcd(width, 512)
    proj_to = proj_v if finish else second_ref

    @pl.loop(0, width // tile)
    def _(i):
        cols = pl.ds(pl.multiple_of(i * tile, tile), tile)
        proj_to[:, cols] = jnp.dot(
            att_ref[...], w_vmem[:, cols], preferred_element_type=jnp.float32
        )

    @pl.loop(1, lead)
    def _(l):
        kv_copy(me, z_send.at[l], ((z + l) % lead) * 8 + low).wait_send()

    @pl.loop(0, lead)
    def _(l):
        base = ((z + l) % lead) * 8
        for hop in (0, 1, 2):
            kv_copy(base + low, f_send.at[hop, base + low], peers[hop]).wait_send()
        two = base + peers[0] % 8
        for hop in (1, 2):
            kv_copy(two, f_send.at[hop, two], peers[hop]).wait_send()
        for far in (base + across % 8, base + across2 % 8):
            kv_copy(far, f_send.at[2, far], peers[2]).wait_send()

    lines = out_ref.shape[1]
    own_lines = pl.ds(pl.multiple_of(me * lines, lines), lines)
    landed[own_lines, :] = spread[own_lines, :]

    @pl.loop(1, n)
    def _(d):
        source = (me + n - shift(d)) % n
        pltpu.make_async_remote_copy(
            src_ref=out_ref.at[source],
            dst_ref=arrived_ref.at[source],
            send_sem=h_send.at[d],
            recv_sem=h_recv.at[source],
            device_id={"ctx": source},
        ).wait_recv()
        landed[pl.ds(pl.multiple_of(source * lines, lines), lines), :] = arrived_ref[
            source
        ].astype(jnp.float32)

    score_copy.wait()
    rows, held_width = hid.shape
    chunks = held_width // 128
    slots = n * capacity

    def column(c):
        return landed[pl.ds(c, slots, stride=chunks), :]

    place = placement(slots, rows, column(0))
    tally = jnp.zeros((rows, 128), jnp.float32)
    for first in range(0, chunks, 2):
        many = min(2, chunks - first)
        part = jnp.concatenate([column(first + c) for c in range(many)], axis=1)
        part = jnp.dot(place, part.astype(jnp.bfloat16), preferred_element_type=jnp.float32)
        cols = slice(first * 128, (first + many) * 128)
        if finish:
            part = (part + proj_v[:, cols]).astype(jnp.bfloat16)
            scored = part.astype(jnp.float32) * score_w_ref[:, cols]
            for c in range(many):
                tally = tally + scored[:, c * 128 : (c + 1) * 128]
        hidden_ref[:, cols] = part.astype(jnp.bfloat16)
    if finish:
        second_ref[...] = jnp.sum(jnp.transpose(tally), axis=0, keepdims=True)

    @pl.loop(1, n)
    def _(d):
        hidden_copy(d).wait_send()


def on_device(hidden_in, route, queries, keys_values, ancestors, segments, w_out, w_score):
    tok_rows = hidden_in.shape[0]
    half_width = hidden_in.shape[1]
    n = lax.axis_size("ctx")
    capacity = (tok_rows + n - 1) // n + 1
    finish = lax.axis_size("tp") == 1
    lines = capacity * half_width // 128
    key_count = (1 + ancestors.shape[1]) * BLOCK
    vmem = pl.BlockSpec(memory_space=pltpu.VMEM)
    anywhere = pl.BlockSpec(memory_space=pl.ANY)
    dma = pltpu.SemaphoreType.DMA
    wide = (tok_rows, w_out.shape[1])
    hidden, second = pl.pallas_call(
        functools.partial(kernel, n, capacity, finish),
        out_shape=(
            jax.ShapeDtypeStruct((tok_rows, half_width), jnp.bfloat16),
            jax.ShapeDtypeStruct((1, tok_rows) if finish else wide, jnp.float32),
        ),
        in_specs=[pl.BlockSpec(memory_space=pltpu.SMEM)] + [anywhere] * 7,
        out_specs=(vmem, vmem),
        scratch_shapes=[
            pltpu.VMEM((n, lines, 128), jnp.bfloat16),
            pltpu.VMEM((n, lines, 128), jnp.bfloat16),
            pltpu.VMEM((n * lines, 128), jnp.float32),
            pltpu.VMEM((n * lines, 128), jnp.float32),
            pltpu.VMEM(hidden_in.shape, jnp.bfloat16),
            pltpu.VMEM(wide if finish else (8, 128), jnp.float32),
            pltpu.VMEM((n, BLOCK, 2 * HEAD), jnp.bfloat16),
            pltpu.VMEM((key_count, HEAD), jnp.bfloat16),
            pltpu.VMEM((key_count, HEAD), jnp.bfloat16),
            pltpu.VMEM(queries.shape, jnp.bfloat16),
            pltpu.VMEM(w_out.shape, jnp.bfloat16),
            pltpu.VMEM(queries.shape, jnp.bfloat16),
            pltpu.VMEM(keys_values.shape, jnp.bfloat16),
            pltpu.VMEM((1, tok_rows), jnp.int32),
            pltpu.VMEM((1, tok_rows), jnp.int32),
            pltpu.VMEM((1, w_score.shape[0]), jnp.float32),
            dma,
            dma((6,)),
            dma((n,)),
            dma((n,)),
            dma((n // 8,)),
            dma((3, n)),
            dma((n,)),
        ],
        compiler_params=pltpu.CompilerParams(
            collective_id=0, has_side_effects=True, vmem_limit_bytes=60 * 1024 * 1024
        ),
    )(
        ancestors,
        queries,
        keys_values,
        route.reshape(1, tok_rows),
        segments.reshape(1, tok_rows),
        w_score.reshape(1, w_score.shape[0]),
        hidden_in,
        w_out,
    )
    if finish:
        return (hidden, second.reshape(tok_rows))
    projected = lax.psum_scatter(second, "tp", scatter_dimension=1, tiled=True)
    hidden_out = (hidden.astype(jnp.float32) + projected).astype(jnp.bfloat16)
    score_part = jnp.sum(hidden_out.astype(jnp.float32) * w_score[None, :], axis=1)
    return (hidden_out, lax.psum(score_part, "tp"))


def solution(mesh):
    placed = (
        P(("group", "ctx"), "tp"),
        P(("group", "ctx")),
        P(("group", "ctx"), "tp"),
        P(("group", "ctx"), None),
        P(("group", "ctx"), None),
        P(("group", "ctx")),
        P("tp", None),
        P("tp"),
    )
    return jax.shard_map(
        on_device,
        mesh=mesh,
        in_specs=placed,
        out_specs=(P(("group", "ctx"), "tp"), P(("group", "ctx"))),
        check_vma=False,
    )
```
